32 devices in a mesh: grp: 2 (over y), lon: 2 (over x), lat: 4 (over z), lev: 2 (over core).
Axes of the slice: x: 2, y: 2, z: 4, core: 2. Of those that a mesh axis runs over, the one named last changes fastest.
Arguments:
- state: bfloat16 [16, 8, 96, 4, 256], P(('grp', 'lat'), 'lon', 'lev'), parts along dimension 0, may hold values from -6 to 6
- adj_in: bfloat16 [16, 8, 2, 96, 4, 128], P(('grp', 'lat'), 'lon', None, 'lev'), parts along dimension 0, may hold values from -6 to 6
- weights: bfloat16 [16, 8, 2, 128, 256], P(('grp', 'lat'), 'lon'), parts along dimension 0, may hold values from -0.5 to 0.5
- slopes: bfloat16 [16, 8, 2, 128, 256], P(('grp', 'lat'), 'lon'), parts along dimension 0, may hold values from -0.01953125 to 0.01953125
- dep_lat: int32 [16, 8, 2], P(('grp', 'lat'), 'lon'), parts along dimension 0, may hold values from -2 to 2, as said below
- dep_lon: int32 [16, 8, 2], P(('grp', 'lat'), 'lon'), parts along dimension 0, may hold values from -2 to 2, as said below
Outputs:
- src_adj: float32 [16, 8, 96, 4, 256], P(('grp', 'lat'), 'lon', 'lev'), parts along dimension 0
- wind_adj: float32 [16, 8, 2, 128], P(('grp', 'lat'), 'lon'), parts along dimension 0
The draws below stay inside these ranges and needn't reach their ends.
There are 2 independent parts, one for each index of `grp`. The reference program is written for one: setup_inputs(seed, part) draws one part's arguments, and reference() takes and returns one part's arrays. A program takes and returns all parts, laid end to end along the dimension named above; each array names one. Nothing has to cross between parts.
Inputs may be any that keep to these rules, and one draw needn't show every extreme that they name: row + dep_lat stays within 0 to 7. |dep_lon| is at most 2 in the rows of the first and last quarter of latitudes and at most 1 elsewhere; longitude wraps around.
All inputs are finite; a program needn't handle non-finite values.
Results may differ from the reference program's by a relative error of at most 0.0003.
Values may be sent and summed in bfloat16 or wider, within the bound.
A program may use at most 64 MiB of HBM per device.

```python
import jax
import jax.numpy as jnp
from jax import lax

LEVELS = 96
FIELDS = 4
CELLS = 256
PTS = 128
TPB = 2
HW = 2
BLAT = 8
BLON = 8


def draw_dep_lat(key, part):
    key = jax.random.fold_in(key, 11)
    step = jax.random.randint(key, (BLAT, BLON, TPB), -HW, HW + 1)
    step = step.at[:, 0, 0].set(-HW).at[:, 0, 1].set(HW)
    rows = jnp.arange(BLAT, dtype=jnp.int32)[:, None, None]
    return (jnp.clip(rows + step, 0, BLAT - 1) - rows).astype(jnp.int32)


def draw_dep_lon(key, part):
    key = jax.random.fold_in(key, 23)
    rows = jnp.arange(BLAT, dtype=jnp.int32)[:, None, None]
    polar = (rows < BLAT // 4) | (rows >= BLAT - BLAT // 4)
    reach = jnp.where(polar, HW, max(HW // 2, 1)).astype(jnp.int32)
    step = jax.random.randint(key, (BLAT, BLON, TPB), -HW, HW + 1)
    step = jnp.clip(step, -reach, reach)
    step = step.at[:, 1, 0].set(reach[:, 0, 0]).at[:, 1, 1].set(-reach[:, 0, 0])
    return step.astype(jnp.int32)


def level_of(rng, shape, cuts, low, largest):
    loudness, own = 1.0, jax.random.fold_in(rng, 6)
    for position, blocks in cuts:
        steps = jnp.exp(jax.random.uniform(jax.random.fold_in(own, position), (blocks,), jnp.float32, low / len(cuts), largest / len(cuts)))
        loudness = loudness * jnp.repeat(steps, shape[position] // blocks).reshape([-1 if axis == position else 1 for axis in range(len(shape))])
    return loudness


def normal_values(rng, dims, spread, most, split=(), kind=jnp.bfloat16):
    factor_of = level_of(rng, dims, split, -0.22, 0.18) if split else 1.0
    drawn = jax.random.normal(rng, dims, jnp.float32) * spread * factor_of
    return jnp.minimum(jnp.maximum(drawn, -most), most).astype(kind)


def setup_inputs(seed: int = 0, part: int = 0) -> dict:
    seeds = jax.random.split(jax.random.key(seed), 7)
    own_keys = jax.random.split(jax.random.fold_in(seeds[6], part), 7)
    state = normal_values(own_keys[0], (BLAT, BLON, LEVELS, FIELDS, CELLS), 1.0, 6.0, ((0, 4), (1, 2), (2, 2)))
    adj_in = normal_values(own_keys[1], (BLAT, BLON, TPB, LEVELS, FIELDS, PTS), 1.0, 6.0, ((0, 4), (1, 2), (3, 2)))
    weights = normal_values(own_keys[2], (BLAT, BLON, TPB, PTS, CELLS), PTS ** -0.5, 0.5, ((0, 4), (1, 2)))
    slopes = normal_values(own_keys[3], (BLAT, BLON, TPB, PTS, CELLS), (CELLS * LEVELS * FIELDS) ** -0.5, 0.01953125, ((0, 4), (1, 2)))
    dep_lat = draw_dep_lat(jax.random.fold_in(jax.random.fold_in(seeds[6], part), 71), part)
    dep_lon = draw_dep_lon(jax.random.fold_in(jax.random.fold_in(seeds[6], part), 71), part)
    return {"state": state, "adj_in": adj_in, "weights": weights, "slopes": slopes, "dep_lat": dep_lat, "dep_lon": dep_lon}


def reference(state, adj_in, weights, slopes, dep_lat, dep_lon):
    rows = jnp.arange(BLAT, dtype=jnp.int32)[:, None, None]
    cols = jnp.arange(BLON, dtype=jnp.int32)[None, :, None]
    src_row = (rows + dep_lat).astype(jnp.int32)
    src_col = ((cols + dep_lon) % BLON).astype(jnp.int32)

    def one_row(pack):
        adj_row, w_row, s_row, row_idx, col_idx = pack
        picked = state[row_idx, col_idx].astype(jnp.float32)
        deriv = jnp.einsum("bkpc,bklfc->bklfp", s_row.astype(jnp.float32), picked)
        adj_f = adj_row.astype(jnp.float32)
        wind = jnp.sum(deriv * adj_f, axis=(2, 3))
        contrib = jnp.einsum("bklfp,bkpc->bklfc", adj_f, w_row.astype(jnp.float32))
        return wind, contrib

    wind_adj, contrib = lax.map(one_row, (adj_in, weights, slopes, src_row, src_col))
    src_adj = jnp.zeros(state.shape, jnp.float32).at[src_row, src_col].add(contrib)
    return src_adj, wind_adj
```

```python
import functools

import jax
import jax.numpy as jnp
from jax import lax
from jax.experimental import pallas as pl
from jax.experimental.pallas import tpu as pltpu
from jax.sharding import PartitionSpec as P

HW = 2
MESH = pl.DeviceIdType.MESH
REGION = 16


def with_halo(array, sides, width, wrap):
    for axis, dim in sides:
        peers, length = (lax.axis_size(axis), array.shape[dim])
        up = [(i, (i + 1) % peers) for i in range(peers if wrap else peers - 1)]
        down = [(j, i) for i, j in up]
        last = lax.slice_in_dim(array, length - width, length, axis=dim)
        initial = lax.slice_in_dim(array, 0, width, axis=dim)
        before = lax.ppermute(last, axis, up)
        after = lax.ppermute(initial, axis, down)
        array = jnp.concatenate([before, array, after], axis=dim)
    return array


def fold_lon(buffer):
    rims = jnp.concatenate([buffer[:, :HW], buffer[:, -HW:]], axis=1)
    got = with_halo(rims, (("lon", 1),), HW, True)
    middle = buffer[:, HW:-HW]
    middle = middle.at[:, :HW].add(got[:, :HW])
    middle = middle.at[:, -HW:].add(got[:, -HW:])
    return middle


def fold_lat(buffer):
    rims = jnp.concatenate([buffer[:HW], buffer[-HW:]], axis=0)
    got = with_halo(rims, (("lat", 0),), HW, False)
    middle = buffer[HW:-HW]
    middle = middle.at[:HW].add(got[:HW])
    middle = middle.at[-HW:].add(got[-HW:])
    return middle


def halo_path(state, adj_in, weights, slopes, dep_lat, dep_lon):
    rows_dev, cols_dev, levels_dev, fields, cells = state.shape
    tiles_blk = adj_in.shape[2]
    points = adj_in.shape[-1]
    channels = levels_dev * fields
    ntile = rows_dev * cols_dev * tiles_blk
    tall = rows_dev + 2 * HW
    wide = cols_dev + 2 * HW
    extended = with_halo(state, (("lat", 0), ("lon", 1)), HW, True)
    blocks = extended.reshape(tall * wide, channels, cells)
    row_ids = jnp.arange(rows_dev, dtype=jnp.int32)[:, None, None]
    col_ids = jnp.arange(cols_dev, dtype=jnp.int32)[None, :, None]
    target = ((row_ids + HW + dep_lat) * wide + col_ids + HW + dep_lon).reshape(ntile)
    picked = blocks[target]
    slope_flat = slopes.reshape(ntile, points, cells)
    weight_flat = weights.reshape(ntile, points, cells)
    adj_flat = adj_in.reshape(ntile, channels, points)
    deriv = jnp.einsum("tpc,tmc->tmp", slope_flat, picked, preferred_element_type=jnp.float32)
    partial_wind = jnp.sum(deriv * adj_flat.astype(jnp.float32), axis=1)
    wind = lax.psum(partial_wind, "lev")
    contrib = jnp.einsum("tmp,tpc->tmc", adj_flat, weight_flat, preferred_element_type=jnp.float32)
    summed = jax.ops.segment_sum(
        contrib.reshape(ntile, channels * cells), target, num_segments=tall * wide
    )
    summed = summed.reshape(tall, wide, channels, cells)
    owned = fold_lat(fold_lon(summed))
    return owned.reshape(rows_dev * cols_dev, channels, cells), wind


class Plan:
    def __init__(self, mesh, ntile):
        self.nlat, self.nlon = mesh.shape["lat"], mesh.shape["lon"]
        lons = (0, 1) if self.nlon == 2 else (0, 1, -1)
        self.near = [(a, b) for b in lons for a in (-1, 1, 0) if (a, b) != (0, 0)]
        self.near.sort(key=lambda d: -(abs(d[0]) + abs(d[1])))
        self.caps, self.bases, self.chunks = [], [], []
        for a, b in self.near:
            cap = 5 if a and b else (8 if b else 9)
            self.bases.append(sum(self.caps))
            self.caps.append(cap)
            self.chunks.append([(0, 4, False), (4, 4, True)] if b and not a else [(0, cap, False)])
        self.slots = sum(self.caps)
        self.count = len(self.near)

    def polar(self, lat):
        quarter = max(self.nlat // 4, 1)
        return (lat < quarter) | (lat >= self.nlat - quarter)

    def exists(self, lat, step):
        if step == 0:
            return lat >= 0
        return (lat + step >= 0) & (lat + step < self.nlat)

    def device(self, step, sign=1, core=None):
        a, b = step
        lat = lax.axis_index("lat") + sign * a
        lon = lax.rem(lax.axis_index("lon") + sign * b + self.nlon, self.nlon)
        core = lax.axis_index("lev") if core is None else core
        return (lax.axis_index("grp"), lon, lat, core)


def index_of_axes(mesh, named):
    order = {"grp": 0, "lon": 1, "lat": 2, "lev": 3}
    return tuple(named[order[a]] for a in mesh.axis_names)


def pack_kernel(
    plan, dims, dlat, dlon, adj, wts, slp, padj, pwts, pslp, dest, own, slot, over, fill, sems
):
    rows, cols, tpb, half = dims
    lat, core = lax.axis_index("lat"), lax.axis_index("lev")
    for k in range(plan.count):
        fill[k] = 0
        for s in range(REGION):
            dest[k, s] = -1
    over[0] = 0
    ntile = rows * cols * tpb

    def copies(t, at):
        rowsl = pl.ds(pl.multiple_of(core * half, half), half)
        return [
            pltpu.make_async_copy(wts.at[t, rowsl], pwts.at[at], sems.at[t, 0]),
            pltpu.make_async_copy(slp.at[t, rowsl], pslp.at[at], sems.at[t, 1]),
            pltpu.make_async_copy(adj.at[t], padj.at[at], sems.at[t, 2]),
        ]

    def place(t, _):
        r = t // (cols * tpb)
        c = lax.rem(t // tpb, cols)
        sr, sc = r + dlat[t], c + dlon[t]
        a = jnp.where(sr < 0, -1, jnp.where(sr >= rows, 1, 0))
        b = jnp.where(sc < 0, -1, jnp.where(sc >= cols, 1, 0))
        block = (sr - a * rows) * cols + sc - b * cols
        if plan.nlon == 2:
            b = jnp.abs(b)
        home = (a == 0) & (b == 0)
        own[t] = jnp.where(home, block, -1)

        @pl.when(home)
        def _():
            slot[t] = plan.count * REGION + t
            fill[plan.count + t] = -1

        for k, (x, y) in enumerate(plan.near):

            @pl.when((a == x) & (b == y))
            def _(k=k, x=x, y=y):
                pos = fill[k]
                fill[k] = pos + 1
                room = plan.caps[k]
                if y and not x:
                    room = jnp.where(plan.polar(lat), room, 4)
                fits = pos < room
                at = jnp.where(fits, pos, 0)
                slot[t] = k * REGION + at
                fill[plan.count + t] = jnp.where(fits, plan.bases[k] + at, -1)

                @pl.when(fits)
                def _():
                    dest[k, at] = block
                    for copy in copies(t, plan.bases[k] + at):
                        copy.start()

                @pl.when(~fits)
                def _():
                    over[0] = 1

        return 0

    lax.fori_loop(0, ntile, place, 0)

    def finish(t, _):
        at = fill[plan.count + t]

        @pl.when(at >= 0)
        def _():
            for copy in copies(t, at):
                copy.wait()

        return 0

    lax.fori_loop(0, ntile, finish, 0)


def send_kernel(
    plan, mesh, padj, pwts, pslp, pdest, radj, rwts, rslp, rdest, ssem, rsem, fsem, gsem
):
    lat, core = lax.axis_index("lat"), lax.axis_index("lev")
    polar = plan.polar(lat)
    partner = index_of_axes(
        mesh, (lax.axis_index("grp"), lax.axis_index("lon"), lat, 1 - core)
    )
    barrier = pltpu.get_barrier_semaphore()
    expected = 1
    pl.semaphore_signal(barrier, inc=1, device_id=partner, device_id_type=MESH)
    for step in plan.near:
        there = plan.exists(lat, step[0])
        expected = expected + there.astype(jnp.int32)

        @pl.when(there)
        def _(step=step):
            pl.semaphore_signal(
                barrier, inc=1, device_id=index_of_axes(mesh, plan.device(step)), device_id_type=MESH
            )

    pl.semaphore_wait(barrier, expected)

    def groups():
        n = 0
        for k, step in enumerate(plan.near):
            for off, size, far in plan.chunks[k]:
                rows = pl.ds(plan.bases[k] + off, size)
                send, get = plan.exists(lat, step[0]), plan.exists(lat, -step[0])
                if far:
                    send, get = send & polar, get & polar
                yield n, k, step, off, rows, send, get
                n += 1

    def outgoing(n, step, rows):
        device = index_of_axes(mesh, plan.device(step))
        pairs = [
            (pwts.at[rows], rwts.at[rows, core]),
            (pslp.at[rows], rslp.at[rows, core]),
            (padj.at[rows], radj.at[rows]),
        ]
        return [
            pltpu.make_async_remote_copy(
                src_ref=src, dst_ref=dst, send_sem=ssem.at[n, j], recv_sem=rsem.at[n, j],
                device_id=device, device_id_type=MESH,
            )
            for j, (src, dst) in enumerate(pairs)
        ]

    def table(k, step):
        return pltpu.make_async_remote_copy(
            src_ref=pdest.at[k], dst_ref=rdest.at[k],
            send_sem=ssem.at[plan.copies + k, 0], recv_sem=rsem.at[plan.copies + k, 0],
            device_id=index_of_axes(mesh, plan.device(step)), device_id_type=MESH,
        )

    def passed(n, rows):
        return [
            pltpu.make_async_remote_copy(
                src_ref=ref.at[rows, core], dst_ref=ref.at[rows, core],
                send_sem=fsem.at[n, j], recv_sem=gsem.at[n, j],
                device_id=partner, device_id_type=MESH,
            )
            for j, ref in enumerate((rwts, rslp))
        ]

    for n, k, step, off, rows, send, get in groups():

        @pl.when(send)
        def _():
            if off == 0:
                table(k, step).start()
            for copy in outgoing(n, step, rows):
                copy.start()

    for n, k, step, off, rows, send, get in groups():

        @pl.when(get)
        def _():
            arrive, on = outgoing(n, step, rows), passed(n, rows)
            for j in range(2):
                arrive[j].wait_recv()
                on[j].start()

    for n, k, step, off, rows, send, get in groups():

        @pl.when(get)
        def _():
            if off == 0:
                table(k, step).wait_recv()
            outgoing(n, step, rows)[2].wait_recv()
            for copy in passed(n, rows):
                copy.wait()

        @pl.when(send)
        def _():
            if off == 0:
                table(k, step).wait_send()
            for copy in outgoing(n, step, rows):
                copy.wait_send()


def work_kernel(
    plan, own, rdest, state, adj, wts, slp, radj, rwts, rslp, src_adj, wind
):
    src_adj[...] = jnp.zeros_like(src_adj)
    wind[...] = jnp.zeros_like(wind)

    def tile(block, t, row, a_ref, w_ref, s_ref):
        @pl.when(block >= 0)
        def _():
            a = a_ref[t]
            src_adj[block] += jnp.dot(a, w_ref[t], preferred_element_type=jnp.float32)
            deriv = lax.dot_general(
                state[block], s_ref[t], (((1,), (1,)), ((), ())),
                preferred_element_type=jnp.float32,
            )
            wind[row] = jnp.sum(deriv * a.astype(jnp.float32), axis=0, keepdims=True)

    def local(t, _):
        tile(own[t], t, plan.count * REGION + t, adj, wts, slp)
        return 0

    lax.fori_loop(0, adj.shape[0], local, 0)
    for k in range(plan.count):

        def arrived(t, _, k=k):
            tile(rdest[k, t], plan.bases[k] + t, k * REGION + t, radj, rwts, rslp)
            return 0

        lax.fori_loop(0, plan.caps[k], arrived, 0)


def wind_kernel(plan, mesh, ntile, slot, wind, out, held, ssem, rsem):
    lat, core = lax.axis_index("lat"), lax.axis_index("lev")
    held[...] = jnp.zeros_like(held)
    here = (lax.axis_index("grp"), lax.axis_index("lon"), lat)
    partner = index_of_axes(mesh, here + (1 - core,))
    barrier = pltpu.get_barrier_semaphore()
    pl.semaphore_signal(barrier, inc=1, device_id=partner, device_id_type=MESH)
    expected = 1
    for step in plan.near:
        there = plan.exists(lat, step[0])
        expected = expected + 2 * there.astype(jnp.int32)

        @pl.when(there)
        def _(step=step):
            for c in range(2):
                pl.semaphore_signal(
                    barrier, inc=1,
                    device_id=index_of_axes(mesh, plan.device(step, 1, c)), device_id_type=MESH,
                )

    pl.semaphore_wait(barrier, expected)

    def back(k, step, c):
        rows = pl.ds(k * REGION, REGION)
        to = core if c == 0 else 1 - core
        return pltpu.make_async_remote_copy(
            src_ref=wind.at[rows], dst_ref=held.at[core, rows],
            send_sem=ssem.at[k, c], recv_sem=rsem.at[k, c],
            device_id=index_of_axes(mesh, plan.device(step, -1, to)), device_id_type=MESH,
        )

    mine = pl.ds(plan.count * REGION, ntile)
    across = pltpu.make_async_remote_copy(
        src_ref=wind.at[mine], dst_ref=held.at[core, mine],
        send_sem=ssem.at[plan.count, 0], recv_sem=rsem.at[plan.count, 0],
        device_id=partner, device_id_type=MESH,
    )
    for k, step in enumerate(plan.near):

        @pl.when(plan.exists(lat, -step[0]))
        def _(k=k, step=step):
            for c in range(2):
                back(k, step, c).start()

    across.start()
    held[core, mine] = wind[mine]
    across.wait()
    for k, step in enumerate(plan.near):

        @pl.when(plan.exists(lat, step[0]))
        def _(k=k, step=step):
            for c in range(2):
                back(k, step, c).wait_recv()

        @pl.when(plan.exists(lat, -step[0]))
        def _(k=k, step=step):
            for c in range(2):
                back(k, step, c).wait_send()

    for t in range(ntile):
        out[t] = held[0, slot[t]] + held[1, slot[t]]


def on_device(mesh, state, adj_in, weights, slopes, dep_lat, dep_lon):
    rows, cols, levels, fields, cells = state.shape
    tpb, points = adj_in.shape[2], adj_in.shape[-1]
    channels, ntile, half = levels * fields, rows * cols * tpb, points // 2
    plan = Plan(mesh, ntile)
    plan.copies = sum(len(c) for c in plan.chunks)
    f32, bf16, i32 = jnp.float32, jnp.bfloat16, jnp.int32
    shape = jax.ShapeDtypeStruct
    anyref = pl.BlockSpec(memory_space=pl.ANY)
    smem = pl.BlockSpec(memory_space=pltpu.SMEM)
    vmem = pl.BlockSpec(memory_space=pltpu.VMEM)
    params = functools.partial(pltpu.CompilerParams, vmem_limit_bytes=48 * 2**20)

    st = state.reshape(rows * cols, channels, cells)
    adj = adj_in.reshape(ntile, channels, points)
    wts = weights.reshape(ntile, points, cells)
    slp = slopes.reshape(ntile, points, cells)

    padj, pwts, pslp, dest, own, slot, over = pl.pallas_call(
        functools.partial(pack_kernel, plan, (rows, cols, tpb, half)),
        out_shape=(
            shape((plan.slots, channels, points), bf16),
            shape((plan.slots, half, cells), bf16),
            shape((plan.slots, half, cells), bf16),
            shape((plan.count, REGION), i32),
            shape((ntile,), i32),
            shape((ntile,), i32),
            shape((1,), i32),
        ),
        in_specs=[smem, smem, anyref, anyref, anyref],
        out_specs=(anyref, anyref, anyref, smem, smem, smem, smem),
        scratch_shapes=[pltpu.SMEM((plan.count + ntile,), i32), pltpu.SemaphoreType.DMA((ntile, 3))],
        compiler_params=params(),
        name="pack",
    )(dep_lat.reshape(ntile), dep_lon.reshape(ntile), adj, wts, slp)

    any_over = lax.psum(over.astype(f32), mesh.axis_names)[0] > 0
    tables = jnp.broadcast_to(
        jnp.pad(dest, ((0, 0), (0, 128 - REGION)))[:, None, :], (plan.count, 8, 128)
    )
    groups = plan.copies + plan.count
    radj, rwts, rslp, rdest = pl.pallas_call(
        functools.partial(send_kernel, plan, mesh),
        out_shape=(
            shape((plan.slots, channels, points), bf16),
            shape((plan.slots, 2, half, cells), bf16),
            shape((plan.slots, 2, half, cells), bf16),
            shape((plan.count, 8, 128), i32),
        ),
        in_specs=[anyref] * 4,
        out_specs=(anyref,) * 4,
        scratch_shapes=[
            pltpu.SemaphoreType.DMA((groups, 3)),
            pltpu.SemaphoreType.DMA((groups, 3)),
            pltpu.SemaphoreType.DMA((plan.copies, 2)),
            pltpu.SemaphoreType.DMA((plan.copies, 2)),
        ],
        compiler_params=params(collective_id=1, has_side_effects=True),
        name="send_tiles",
    )(padj, pwts, pslp, tables)

    lat = lax.axis_index("lat")
    came = jnp.stack([plan.exists(lat, -a) for a, b in plan.near])
    rdest = jnp.where(came[:, None], rdest[:, 0, :REGION], -1)

    def owner_path(_):
        total = (plan.count * REGION) + ntile
        src_adj, wind = pl.pallas_call(
            functools.partial(work_kernel, plan),
            out_shape=(
                shape((rows * cols, channels, cells), f32),
                shape((total, 1, points), f32),
            ),
            in_specs=[smem, smem] + [vmem] * 7,
            out_specs=(vmem, vmem),
            compiler_params=params(),
            name="tile_products",
        )(
            own, rdest, st, adj, wts, slp, radj,
            rwts.reshape(plan.slots, points, cells), rslp.reshape(plan.slots, points, cells),
        )
        wind = pl.pallas_call(
            functools.partial(wind_kernel, plan, mesh, ntile),
            out_shape=shape((ntile, 1, points), f32),
            in_specs=[smem, vmem],
            out_specs=vmem,
            scratch_shapes=[
                pltpu.VMEM((2, total, 1, points), f32),
                pltpu.SemaphoreType.DMA((plan.count + 1, 2)),
                pltpu.SemaphoreType.DMA((plan.count + 1, 2)),
            ],
            compiler_params=params(collective_id=2, has_side_effects=True),
            name="wind_rows",
        )(slot, wind)
        return src_adj, wind.reshape(ntile, points)

    def general_path(_):
        return halo_path(state, adj_in, weights, slopes, dep_lat, dep_lon)

    src_adj, wind = lax.cond(any_over, general_path, owner_path, 0)
    return (
        src_adj.reshape(rows, cols, levels, fields, cells),
        wind.reshape(rows, cols, tpb, points),
    )


def solution(mesh):
    placed = (
        P(("grp", "lat"), "lon", "lev", None, None),
        P(("grp", "lat"), "lon", None, "lev", None, None),
        P(("grp", "lat"), "lon", None, None, None),
        P(("grp", "lat"), "lon", None, None, None),
        P(("grp", "lat"), "lon", None),
        P(("grp", "lat"), "lon", None),
    )
    return jax.shard_map(
        functools.partial(on_device, mesh),
        mesh=mesh,
        in_specs=placed,
        out_specs=(
            P(("grp", "lat"), "lon", "lev", None, None),
            P(("grp", "lat"), "lon", None, None),
        ),
        check_vma=False,
    )
```

```python
import functools

import jax
import jax.numpy as jnp
from jax import lax
from jax.experimental import pallas as pl
from jax.experimental.pallas import tpu as pltpu
from jax.sharding import PartitionSpec as P

HW = 2
MESH = pl.DeviceIdType.MESH
REGION = 16


def with_halo(array, sides, width, wrap):
    for axis, dim in sides:
        peers, length = (lax.axis_size(axis), array.shape[dim])
        up = [(i, (i + 1) % peers) for i in range(peers if wrap else peers - 1)]
        down = [(j, i) for i, j in up]
        last = lax.slice_in_dim(array, length - width, length, axis=dim)
        initial = lax.slice_in_dim(array, 0, width, axis=dim)
        before = lax.ppermute(last, axis, up)
        after = lax.ppermute(initial, axis, down)
        array = jnp.concatenate([before, array, after], axis=dim)
    return array


def fold_lon(buffer):
    rims = jnp.concatenate([buffer[:, :HW], buffer[:, -HW:]], axis=1)
    got = with_halo(rims, (("lon", 1),), HW, True)
    middle = buffer[:, HW:-HW]
    middle = middle.at[:, :HW].add(got[:, :HW])
    middle = middle.at[:, -HW:].add(got[:, -HW:])
    return middle


def fold_lat(buffer):
    rims = jnp.concatenate([buffer[:HW], buffer[-HW:]], axis=0)
    got = with_halo(rims, (("lat", 0),), HW, False)
    middle = buffer[HW:-HW]
    middle = middle.at[:HW].add(got[:HW])
    middle = middle.at[-HW:].add(got[-HW:])
    return middle


def halo_path(state, adj_in, weights, slopes, dep_lat, dep_lon):
    rows_dev, cols_dev, levels_dev, fields, cells = state.shape
    tiles_blk = adj_in.shape[2]
    points = adj_in.shape[-1]
    channels = levels_dev * fields
    ntile = rows_dev * cols_dev * tiles_blk
    tall = rows_dev + 2 * HW
    wide = cols_dev + 2 * HW
    extended = with_halo(state, (("lat", 0), ("lon", 1)), HW, True)
    blocks = extended.reshape(tall * wide, channels, cells)
    row_ids = jnp.arange(rows_dev, dtype=jnp.int32)[:, None, None]
    col_ids = jnp.arange(cols_dev, dtype=jnp.int32)[None, :, None]
    target = ((row_ids + HW + dep_lat) * wide + col_ids + HW + dep_lon).reshape(ntile)
    picked = blocks[target]
    slope_flat = slopes.reshape(ntile, points, cells)
    weight_flat = weights.reshape(ntile, points, cells)
    adj_flat = adj_in.reshape(ntile, channels, points)
    deriv = jnp.einsum("tpc,tmc->tmp", slope_flat, picked, preferred_element_type=jnp.float32)
    partial_wind = jnp.sum(deriv * adj_flat.astype(jnp.float32), axis=1)
    wind = lax.psum(partial_wind, "lev")
    contrib = jnp.einsum("tmp,tpc->tmc", adj_flat, weight_flat, preferred_element_type=jnp.float32)
    summed = jax.ops.segment_sum(
        contrib.reshape(ntile, channels * cells), target, num_segments=tall * wide
    )
    summed = summed.reshape(tall, wide, channels, cells)
    owned = fold_lat(fold_lon(summed))
    return owned.reshape(rows_dev * cols_dev, levels_dev, fields, cells), wind


class Plan:
    def __init__(self, mesh, ntile):
        self.nlat, self.nlon = mesh.shape["lat"], mesh.shape["lon"]
        lons = (0, 1) if self.nlon == 2 else (0, 1, -1)
        self.near = [(a, b) for b in lons for a in (-1, 1, 0) if (a, b) != (0, 0)]
        self.near.sort(key=lambda d: -(abs(d[0]) + abs(d[1])))
        self.caps, self.bases, self.chunks = [], [], []
        self.rooms = []
        for a, b in self.near:
            edge, inner = (6, 5) if a and b else ((9, 5) if b else (9, 10))
            low, cap = min(edge, inner), max(edge, inner)
            self.bases.append(sum(self.caps))
            self.caps.append(cap)
            self.rooms.append((edge, inner))
            self.chunks.append([(0, low, None), (low, cap - low, edge > inner)])
        self.slots = sum(self.caps)
        self.count = len(self.near)

    def polar(self, lat):
        quarter = max(self.nlat // 4, 1)
        return (lat < quarter) | (lat >= self.nlat - quarter)

    def exists(self, lat, step):
        if step == 0:
            return lat >= 0
        return (lat + step >= 0) & (lat + step < self.nlat)

    def device(self, step, sign=1, core=None):
        a, b = step
        lat = lax.axis_index("lat") + sign * a
        lon = lax.rem(lax.axis_index("lon") + sign * b + self.nlon, self.nlon)
        core = lax.axis_index("lev") if core is None else core
        return (lax.axis_index("grp"), lon, lat, core)


def index_of_axes(mesh, named):
    order = {"grp": 0, "lon": 1, "lat": 2, "lev": 3}
    return tuple(named[order[a]] for a in mesh.axis_names)


def pack_kernel(
    plan, dims, dlat, dlon, adj, wts, slp, padj, pwts, pslp, dest, own, slot, over, fill, sems
):
    rows, cols, tpb, half = dims
    lat, core = lax.axis_index("lat"), lax.axis_index("lev")
    for k in range(plan.count):
        fill[k] = 0
        for s in range(REGION):
            dest[k, s] = -1
    over[0] = 0
    ntile = rows * cols * tpb

    def copies(t, at):
        rowsl = pl.ds(pl.multiple_of(core * half, half), half)
        return [
            pltpu.make_async_copy(wts.at[t, rowsl], pwts.at[at], sems.at[t, 0]),
            pltpu.make_async_copy(slp.at[t, rowsl], pslp.at[at], sems.at[t, 1]),
            pltpu.make_async_copy(adj.at[t], padj.at[at], sems.at[t, 2]),
        ]

    def place(t, _):
        r = t // (cols * tpb)
        c = lax.rem(t // tpb, cols)
        u = lax.rem(t, tpb)
        sr, sc = r + dlat[r, c, u], c + dlon[r, c, u]
        a = jnp.where(sr < 0, -1, jnp.where(sr >= rows, 1, 0))
        b = jnp.where(sc < 0, -1, jnp.where(sc >= cols, 1, 0))
        block = (sr - a * rows) * cols + sc - b * cols
        if plan.nlon == 2:
            b = jnp.abs(b)
        home = (a == 0) & (b == 0)
        own[t] = jnp.where(home, block, -1)

        @pl.when(home)
        def _():
            slot[t] = plan.count * REGION + t
            fill[plan.count + t] = -1

        for k, (x, y) in enumerate(plan.near):

            @pl.when((a == x) & (b == y))
            def _(k=k, x=x, y=y):
                pos = fill[k]
                fill[k] = pos + 1
                room = jnp.where(plan.polar(lat), *plan.rooms[k])
                fits = pos < room
                at = jnp.where(fits, pos, 0)
                slot[t] = k * REGION + at
                fill[plan.count + t] = jnp.where(fits, plan.bases[k] + at, -1)

                @pl.when(fits)
                def _():
                    dest[k, at] = block
                    for copy in copies(t, plan.bases[k] + at):
                        copy.start()

                @pl.when(~fits)
                def _():
                    over[0] = 1

        return 0

    lax.fori_loop(0, ntile, place, 0)

    def finish(t, _):
        at = fill[plan.count + t]

        @pl.when(at >= 0)
        def _():
            for copy in copies(t, at):
                copy.wait()

        return 0

    lax.fori_loop(0, ntile, finish, 0)


def send_kernel(
    plan, mesh, padj, pwts, pslp, pdest, mine, radj, rwts, rslp, rdest, over,
    plane, both, quad, ssem, rsem, fsem, gsem, psem, qsem, usem, vsem,
):
    grp, lon = lax.axis_index("grp"), lax.axis_index("lon")
    lat, core = lax.axis_index("lat"), lax.axis_index("lev")
    ncore = mesh.shape["lev"]
    nplane, nquad = plan.nlon * plan.nlat, mesh.shape["grp"] * ncore
    here, corner = lon * plan.nlat + lat, grp * ncore + core
    polar = plan.polar(lat)
    partner = index_of_axes(mesh, (grp, lon, lat, 1 - core))

    def in_plane(q):
        return index_of_axes(mesh, (grp, q // plan.nlat, lax.rem(q, plan.nlat), core))

    def in_quad(q):
        return index_of_axes(mesh, (q // ncore, lon, lat, lax.rem(q, ncore)))

    def others(count, me, do):
        def step(q, _):
            pl.when(q != me)(lambda: do(q))
            return 0

        lax.fori_loop(0, count, step, 0)

    barrier = pltpu.get_barrier_semaphore()

    def greet(device):
        pl.semaphore_signal(barrier, inc=1, device_id=device, device_id_type=MESH)

    others(nplane, here, lambda q: greet(in_plane(q)))
    others(nquad, corner, lambda q: greet(in_quad(q)))
    pl.semaphore_wait(barrier, nplane + nquad - 2)

    def flag(src, table, me, to, q, send, recv):
        return pltpu.make_async_remote_copy(
            src_ref=src, dst_ref=table.at[me], send_sem=send.at[q], recv_sem=recv.at[me],
            device_id=to(q), device_id_type=MESH,
        )

    def flag_in(src, table, to, q, send, recv):
        return pltpu.make_async_remote_copy(
            src_ref=src, dst_ref=table.at[q], send_sem=send.at[q], recv_sem=recv.at[q],
            device_id=to(q), device_id_type=MESH,
        )

    others(nplane, here, lambda q: flag(mine, plane, here, in_plane, q, psem, qsem).start())
    plane[here] = mine[...]

    def groups():
        n = 0
        for k, step in enumerate(plan.near):
            for off, size, far in plan.chunks[k]:
                rows = pl.ds(plan.bases[k] + off, size)
                send, get = plan.exists(lat, step[0]), plan.exists(lat, -step[0])
                if far is not None:
                    send = send & (polar == far)
                    get = get & (plan.polar(lat - step[0]) == far)
                yield n, k, step, off, rows, send, get
                n += 1

    def outgoing(n, step, rows):
        device = index_of_axes(mesh, plan.device(step))
        pairs = [
            (pwts.at[rows], rwts.at[rows, core]),
            (pslp.at[rows], rslp.at[rows, core]),
            (padj.at[rows], radj.at[rows]),
        ]
        return [
            pltpu.make_async_remote_copy(
                src_ref=src, dst_ref=dst, send_sem=ssem.at[n, j], recv_sem=rsem.at[n, j],
                device_id=device, device_id_type=MESH,
            )
            for j, (src, dst) in enumerate(pairs)
        ]

    def table(k, step):
        return pltpu.make_async_remote_copy(
            src_ref=pdest.at[k], dst_ref=rdest.at[k],
            send_sem=ssem.at[plan.copies + k, 0], recv_sem=rsem.at[plan.copies + k, 0],
            device_id=index_of_axes(mesh, plan.device(step)), device_id_type=MESH,
        )

    def passed(n, rows):
        return [
            pltpu.make_async_remote_copy(
                src_ref=ref.at[rows, core], dst_ref=ref.at[rows, core],
                send_sem=fsem.at[n, j], recv_sem=gsem.at[n, j],
                device_id=partner, device_id_type=MESH,
            )
            for j, ref in enumerate((rwts, rslp))
        ]

    for n, k, step, off, rows, send, get in groups():

        @pl.when(send)
        def _():
            if off == 0:
                table(k, step).start()
            for copy in outgoing(n, step, rows)[:2]:
                copy.start()

    for n, k, step, off, rows, send, get in groups():
        pl.when(send)(lambda: outgoing(n, step, rows)[2].start())

    others(nplane, here, lambda q: flag_in(mine, plane, in_plane, q, psem, qsem).wait_recv())
    both[...] = jnp.max(plane[...], axis=0)
    others(nquad, corner, lambda q: flag(both, quad, corner, in_quad, q, usem, vsem).start())
    quad[corner] = both[...]

    for n, k, step, off, rows, send, get in groups():

        @pl.when(get)
        def _():
            arrive, on = outgoing(n, step, rows), passed(n, rows)
            for j in range(2):
                arrive[j].wait_recv()
                on[j].start()

    others(nquad, corner, lambda q: flag_in(both, quad, in_quad, q, usem, vsem).wait())
    others(nplane, here, lambda q: flag_in(mine, plane, in_plane, q, psem, qsem).wait_send())
    over[0] = jnp.max(quad[...])

    for n, k, step, off, rows, send, get in groups():

        @pl.when(get)
        def _():
            if off == 0:
                table(k, step).wait_recv()
            outgoing(n, step, rows)[2].wait_recv()
            for copy in passed(n, rows):
                copy.wait()

        @pl.when(send)
        def _():
            if off == 0:
                table(k, step).wait_send()
            for copy in outgoing(n, step, rows):
                copy.wait_send()


def work_kernel(
    plan, own, rdest, state, adj, wts, slp, radj, rwts, rslp, src_adj, wind,
    total, adj_in, wts_in, slp_in, sems,
):
    ntile = adj.shape[0]

    def copies(t, at, refs):
        into = (adj_in, wts_in, slp_in)
        return [
            pltpu.make_async_copy(ref.at[t], dst.at[at], sems.at[at, j])
            for j, (ref, dst) in enumerate(zip(refs, into))
        ]

    def begin(block, t, at, refs):
        @pl.when(block >= 0)
        def _():
            for copy in copies(t, at, refs):
                copy.start()

    def tile(block, t, at, row, refs):
        @pl.when(block >= 0)
        def _():
            for copy in copies(t, at, refs):
                copy.wait()
            a = adj_in[at]
            total[block] += jnp.dot(a, wts_in[at], preferred_element_type=jnp.float32)
            deriv = lax.dot_general(
                state[block].reshape(total.shape[1:]), slp_in[at], (((1,), (1,)), ((), ())),
                preferred_element_type=jnp.float32,
            )
            wind[row] = jnp.sum(deriv * a.astype(jnp.float32), axis=0, keepdims=True)

    def every(do):
        def local(t, _):
            do(own[t], t, t, plan.count * REGION + t, (adj, wts, slp))
            return 0

        lax.fori_loop(0, ntile, local, 0)
        for k in range(plan.count):

            def arrived(i, _, k=k):
                t = plan.bases[k] + i
                do(rdest[k, i], t, ntile + t, k * REGION + i, (radj, rwts, rslp))
                return 0

            lax.fori_loop(0, plan.caps[k], arrived, 0)

    every(lambda block, t, at, row, refs: begin(block, t, at, refs))
    total[...] = jnp.zeros_like(total)
    wind[...] = jnp.zeros_like(wind)
    every(tile)

    def give(b, _):
        src_adj[b] = total[b].reshape(src_adj.shape[1:])
        return 0

    lax.fori_loop(0, total.shape[0], give, 0)


def wind_kernel(plan, mesh, ntile, slot, wind, out, held, ssem, rsem):
    lat, core = lax.axis_index("lat"), lax.axis_index("lev")
    held[...] = jnp.zeros_like(held)
    here = (lax.axis_index("grp"), lax.axis_index("lon"), lat)
    partner = index_of_axes(mesh, here + (1 - core,))
    barrier = pltpu.get_barrier_semaphore()
    pl.semaphore_signal(barrier, inc=1, device_id=partner, device_id_type=MESH)
    expected = 1
    for step in plan.near:
        there = plan.exists(lat, step[0])
        expected = expected + 2 * there.astype(jnp.int32)

        @pl.when(there)
        def _(step=step):
            for c in range(2):
                pl.semaphore_signal(
                    barrier, inc=1,
                    device_id=index_of_axes(mesh, plan.device(step, 1, c)), device_id_type=MESH,
                )

    pl.semaphore_wait(barrier, expected)

    def back(k, step, c):
        rows = pl.ds(k * REGION, REGION)
        to = core if c == 0 else 1 - core
        return pltpu.make_async_remote_copy(
            src_ref=wind.at[rows], dst_ref=held.at[core, rows],
            send_sem=ssem.at[k, c], recv_sem=rsem.at[k, c],
            device_id=index_of_axes(mesh, plan.device(step, -1, to)), device_id_type=MESH,
        )

    mine = pl.ds(plan.count * REGION, ntile)
    across = pltpu.make_async_remote_copy(
        src_ref=wind.at[mine], dst_ref=held.at[core, mine],
        send_sem=ssem.at[plan.count, 0], recv_sem=rsem.at[plan.count, 0],
        device_id=partner, device_id_type=MESH,
    )
    for k, step in enumerate(plan.near):

        @pl.when(plan.exists(lat, -step[0]))
        def _(k=k, step=step):
            for c in range(2):
                back(k, step, c).start()

    across.start()
    held[core, mine] = wind[mine]
    across.wait()
    for k, step in enumerate(plan.near):

        @pl.when(plan.exists(lat, step[0]))
        def _(k=k, step=step):
            for c in range(2):
                back(k, step, c).wait_recv()

        @pl.when(plan.exists(lat, -step[0]))
        def _(k=k, step=step):
            for c in range(2):
                back(k, step, c).wait_send()

    for t in range(ntile):
        out[t] = held[0, slot[t]] + held[1, slot[t]]


def on_device(mesh, state, adj_in, weights, slopes, dep_lat, dep_lon):
    rows, cols, levels, fields, cells = state.shape
    tpb, points = adj_in.shape[2], adj_in.shape[-1]
    channels, ntile, half = levels * fields, rows * cols * tpb, points // 2
    plan = Plan(mesh, ntile)
    plan.copies = sum(len(c) for c in plan.chunks)
    f32, bf16, i32 = jnp.float32, jnp.bfloat16, jnp.int32
    shape = jax.ShapeDtypeStruct
    anyref = pl.BlockSpec(memory_space=pl.ANY)
    smem = pl.BlockSpec(memory_space=pltpu.SMEM)
    vmem = pl.BlockSpec(memory_space=pltpu.VMEM)
    params = functools.partial(pltpu.CompilerParams, vmem_limit_bytes=48 * 2**20)

    st = state.reshape(rows * cols, levels, fields, cells)
    adj = adj_in.reshape(ntile, channels, points)
    wts = weights.reshape(ntile, points, cells)
    slp = slopes.reshape(ntile, points, cells)

    padj, pwts, pslp, dest, own, slot, over = pl.pallas_call(
        functools.partial(pack_kernel, plan, (rows, cols, tpb, half)),
        out_shape=(
            shape((plan.slots, channels, points), bf16),
            shape((plan.slots, half, cells), bf16),
            shape((plan.slots, half, cells), bf16),
            shape((plan.count, REGION), i32),
            shape((ntile,), i32),
            shape((ntile,), i32),
            shape((1,), i32),
        ),
        in_specs=[smem, smem, anyref, anyref, anyref],
        out_specs=(anyref, anyref, anyref, smem, smem, smem, smem),
        scratch_shapes=[pltpu.SMEM((plan.count + ntile,), i32), pltpu.SemaphoreType.DMA((ntile, 3))],
        compiler_params=params(),
        name="pack",
    )(dep_lat, dep_lon, adj, wts, slp)

    tables = jnp.broadcast_to(
        jnp.pad(dest, ((0, 0), (0, 128 - REGION)))[:, None, :], (plan.count, 8, 128)
    )
    groups = plan.copies + plan.count
    nplane = plan.nlon * plan.nlat
    nquad = mesh.shape["grp"] * mesh.shape["lev"]
    dma = pltpu.SemaphoreType.DMA
    radj, rwts, rslp, rdest, over = pl.pallas_call(
        functools.partial(send_kernel, plan, mesh),
        out_shape=(
            shape((plan.slots, channels, points), bf16),
            shape((plan.slots, 2, half, cells), bf16),
            shape((plan.slots, 2, half, cells), bf16),
            shape((plan.count, 8, 128), i32),
            shape((1,), i32),
        ),
        in_specs=[anyref] * 4 + [vmem],
        out_specs=(anyref,) * 4 + (smem,),
        scratch_shapes=[
            pltpu.VMEM((nplane, 8, 128), i32),
            pltpu.VMEM((8, 128), i32),
            pltpu.VMEM((nquad, 8, 128), i32),
            pltpu.SemaphoreType.DMA((groups, 3)),
            pltpu.SemaphoreType.DMA((groups, 3)),
            pltpu.SemaphoreType.DMA((plan.copies, 2)),
            pltpu.SemaphoreType.DMA((plan.copies, 2)),
            dma((nplane,)), dma((nplane,)), dma((nquad,)), dma((nquad,)),
        ],
        compiler_params=params(collective_id=1, has_side_effects=True),
        name="send_tiles",
    )(padj, pwts, pslp, tables, jnp.broadcast_to(over, (8, 128)))

    lat = lax.axis_index("lat")
    came = jnp.stack([plan.exists(lat, -a) for a, b in plan.near])
    rdest = jnp.where(came[:, None], rdest[:, 0, :REGION], -1)

    def owner_path(_):
        total = (plan.count * REGION) + ntile
        src_adj, wind = pl.pallas_call(
            functools.partial(work_kernel, plan),
            out_shape=(
                shape((rows * cols, levels, fields, cells), f32),
                shape((total, 1, points), f32),
            ),
            in_specs=[smem, smem, vmem] + [anyref] * 6,
            out_specs=(vmem, vmem),
            scratch_shapes=[
                pltpu.VMEM((rows * cols, channels, cells), f32),
                pltpu.VMEM((ntile + plan.slots, channels, points), bf16),
                pltpu.VMEM((ntile + plan.slots, points, cells), bf16),
                pltpu.VMEM((ntile + plan.slots, points, cells), bf16),
                dma((ntile + plan.slots, 3)),
            ],
            compiler_params=params(),
            name="tile_products",
        )(
            own, rdest, st, adj, wts, slp, radj,
            rwts.reshape(plan.slots, points, cells), rslp.reshape(plan.slots, points, cells),
        )
        wind = pl.pallas_call(
            functools.partial(wind_kernel, plan, mesh, ntile),
            out_shape=shape((ntile, 1, points), f32),
            in_specs=[smem, vmem],
            out_specs=vmem,
            scratch_shapes=[
                pltpu.VMEM((2, total, 1, points), f32),
                pltpu.SemaphoreType.DMA((plan.count + 1, 2)),
                pltpu.SemaphoreType.DMA((plan.count + 1, 2)),
            ],
            compiler_params=params(collective_id=2, has_side_effects=True),
            name="wind_rows",
        )(slot, wind)
        return src_adj, wind.reshape(ntile, points)

    def general_path(_):
        return halo_path(state, adj_in, weights, slopes, dep_lat, dep_lon)

    src_adj, wind = lax.cond(over[0] > 0, general_path, owner_path, 0)
    return (
        src_adj.reshape(rows, cols, levels, fields, cells),
        wind.reshape(rows, cols, tpb, points),
    )


def solution(mesh):
    placed = (
        P(("grp", "lat"), "lon", "lev", None, None),
        P(("grp", "lat"), "lon", None, "lev", None, None),
        P(("grp", "lat"), "lon", None, None, None),
        P(("grp", "lat"), "lon", None, None, None),
        P(("grp", "lat"), "lon", None),
        P(("grp", "lat"), "lon", None),
    )
    return jax.shard_map(
        functools.partial(on_device, mesh),
        mesh=mesh,
        in_specs=placed,
        out_specs=(
            P(("grp", "lat"), "lon", "lev", None, None),
            P(("grp", "lat"), "lon", None, None),
        ),
        check_vma=False,
    )
```

```python
import functools

import jax
import jax.numpy as jnp
from jax import lax
from jax.experimental import pallas as pl
from jax.experimental.pallas import tpu as pltpu
from jax.sharding import PartitionSpec as P

HW = 2
MESH = pl.DeviceIdType.MESH
REGION = 16


def with_halo(array, sides, width, wrap):
    for axis, dim in sides:
        peers, length = (lax.axis_size(axis), array.shape[dim])
        up = [(i, (i + 1) % peers) for i in range(peers if wrap else peers - 1)]
        down = [(j, i) for i, j in up]
        last = lax.slice_in_dim(array, length - width, length, axis=dim)
        initial = lax.slice_in_dim(array, 0, width, axis=dim)
        before = lax.ppermute(last, axis, up)
        after = lax.ppermute(initial, axis, down)
        array = jnp.concatenate([before, array, after], axis=dim)
    return array


def fold_lon(buffer):
    rims = jnp.concatenate([buffer[:, :HW], buffer[:, -HW:]], axis=1)
    got = with_halo(rims, (("lon", 1),), HW, True)
    middle = buffer[:, HW:-HW]
    middle = middle.at[:, :HW].add(got[:, :HW])
    middle = middle.at[:, -HW:].add(got[:, -HW:])
    return middle


def fold_lat(buffer):
    rims = jnp.concatenate([buffer[:HW], buffer[-HW:]], axis=0)
    got = with_halo(rims, (("lat", 0),), HW, False)
    middle = buffer[HW:-HW]
    middle = middle.at[:HW].add(got[:HW])
    middle = middle.at[-HW:].add(got[-HW:])
    return middle


def halo_path(state, adj_in, weights, slopes, dep_lat, dep_lon):
    rows_dev, cols_dev, levels_dev, fields, cells = state.shape
    tiles_blk = adj_in.shape[2]
    points = adj_in.shape[-1]
    channels = levels_dev * fields
    ntile = rows_dev * cols_dev * tiles_blk
    tall = rows_dev + 2 * HW
    wide = cols_dev + 2 * HW
    extended = with_halo(state, (("lat", 0), ("lon", 1)), HW, True)
    blocks = extended.reshape(tall * wide, channels, cells)
    row_ids = jnp.arange(rows_dev, dtype=jnp.int32)[:, None, None]
    col_ids = jnp.arange(cols_dev, dtype=jnp.int32)[None, :, None]
    target = ((row_ids + HW + dep_lat) * wide + col_ids + HW + dep_lon).reshape(ntile)
    picked = blocks[target]
    slope_flat = slopes.reshape(ntile, points, cells)
    weight_flat = weights.reshape(ntile, points, cells)
    adj_flat = adj_in.reshape(ntile, channels, points)
    deriv = jnp.einsum("tpc,tmc->tmp", slope_flat, picked, preferred_element_type=jnp.float32)
    partial_wind = jnp.sum(deriv * adj_flat.astype(jnp.float32), axis=1)
    wind = lax.psum(partial_wind, "lev")
    contrib = jnp.einsum("tmp,tpc->tmc", adj_flat, weight_flat, preferred_element_type=jnp.float32)
    summed = jax.ops.segment_sum(
        contrib.reshape(ntile, channels * cells), target, num_segments=tall * wide
    )
    summed = summed.reshape(tall, wide, channels, cells)
    owned = fold_lat(fold_lon(summed))
    return owned.reshape(rows_dev * cols_dev, levels_dev, fields, cells), wind


class Plan:
    def __init__(self, mesh, ntile):
        self.nlat, self.nlon = mesh.shape["lat"], mesh.shape["lon"]
        lons = (0, 1) if self.nlon == 2 else (0, 1, -1)
        self.near = [(a, b) for b in lons for a in (-1, 1, 0) if (a, b) != (0, 0)]
        self.near.sort(key=lambda d: -(abs(d[0]) + abs(d[1])))
        self.caps, self.bases, self.chunks = [], [], []
        self.rooms = []
        for a, b in self.near:
            edge, inner = (6, 5) if a and b else ((9, 5) if b else (9, 10))
            low, cap = min(edge, inner), max(edge, inner)
            self.bases.append(sum(self.caps))
            self.caps.append(cap)
            self.rooms.append((edge, inner))
            self.chunks.append([(0, low, None), (low, cap - low, edge > inner)])
        self.slots = sum(self.caps)
        self.count = len(self.near)

    def polar(self, lat):
        quarter = max(self.nlat // 4, 1)
        return (lat < quarter) | (lat >= self.nlat - quarter)

    def exists(self, lat, step):
        if step == 0:
            return lat >= 0
        return (lat + step >= 0) & (lat + step < self.nlat)

    def device(self, step, sign=1, core=None):
        a, b = step
        lat = lax.axis_index("lat") + sign * a
        lon = lax.rem(lax.axis_index("lon") + sign * b + self.nlon, self.nlon)
        core = lax.axis_index("lev") if core is None else core
        return (lax.axis_index("grp"), lon, lat, core)


def index_of_axes(mesh, named):
    order = {"grp": 0, "lon": 1, "lat": 2, "lev": 3}
    return tuple(named[order[a]] for a in mesh.axis_names)


def pack_kernel(
    plan, dims, moved, adj, wts, slp, padj, pwts, pslp, dest, own, slot, mine, over, fill, sems
):
    rows, cols, tpb, half = dims
    lat, core = lax.axis_index("lat"), lax.axis_index("lev")
    for k in range(plan.count):
        fill[k] = 0
        for s in range(REGION + 1):
            dest[k, s] = 0
    over[0] = 0
    ntile = rows * cols * tpb

    def copies(t, at):
        rowsl = pl.ds(pl.multiple_of(core * half, half), half)
        return [
            pltpu.make_async_copy(wts.at[t, rowsl], pwts.at[at], sems.at[t, 0]),
            pltpu.make_async_copy(slp.at[t, rowsl], pslp.at[at], sems.at[t, 1]),
            pltpu.make_async_copy(adj.at[t], padj.at[at], sems.at[t, 2]),
        ]

    def place(t, _):
        r = t // (cols * tpb)
        c = lax.rem(t // tpb, cols)
        u = lax.rem(t, tpb)
        code = moved[r, c, u]
        sr, sc = r + code // 8 - HW, c + lax.rem(code, 8) - HW
        a = jnp.where(sr < 0, -1, jnp.where(sr >= rows, 1, 0))
        b = jnp.where(sc < 0, -1, jnp.where(sc >= cols, 1, 0))
        block = (sr - a * rows) * cols + sc - b * cols
        if plan.nlon == 2:
            b = jnp.abs(b)
        home = (a == 0) & (b == 0)
        own[t] = jnp.where(home, block, -1)

        @pl.when(home)
        def _():
            slot[t] = plan.count * REGION + t
            fill[plan.count + t] = -1

        for k, (x, y) in enumerate(plan.near):

            @pl.when((a == x) & (b == y))
            def _(k=k, x=x, y=y):
                pos = fill[k]
                fill[k] = pos + 1
                room = jnp.where(plan.polar(lat), *plan.rooms[k])
                fits = pos < room
                at = jnp.where(fits, pos, 0)
                slot[t] = k * REGION + at
                fill[plan.count + t] = jnp.where(fits, plan.bases[k] + at, -1)

                @pl.when(fits)
                def _():
                    dest[k, at] = block
                    dest[k, REGION] = at + 1
                    for copy in copies(t, plan.bases[k] + at):
                        copy.start()

                @pl.when(~fits)
                def _():
                    over[0] = 1

        return 0

    lax.fori_loop(0, ntile, place, 0)

    def finish(t, _):
        at = fill[plan.count + t]

        @pl.when(at >= 0)
        def _():
            for copy in copies(t, at):
                copy.wait()

        return 0

    lax.fori_loop(0, ntile, finish, 0)
    mine[...] = jnp.full(mine.shape, over[0], jnp.int32)


def send_kernel(
    plan, mesh, padj, pwts, pslp, pdest, mine, own, state, adj, wts, slp,
    radj, rwts, rslp, rdest, over, home, wind,
    st_in, adj_in, wts_in, slp_in, total, lsem, plane, both, quad, ssem, rsem, fsem, gsem, psem, qsem, usem, vsem,
):
    grp, lon = lax.axis_index("grp"), lax.axis_index("lon")
    lat, core = lax.axis_index("lat"), lax.axis_index("lev")
    ncore = mesh.shape["lev"]
    nplane, nquad = plan.nlon * plan.nlat, mesh.shape["grp"] * ncore
    here, corner = lon * plan.nlat + lat, grp * ncore + core
    polar = plan.polar(lat)
    partner = index_of_axes(mesh, (grp, lon, lat, 1 - core))

    def in_plane(q):
        return index_of_axes(mesh, (grp, q // plan.nlat, lax.rem(q, plan.nlat), core))

    def in_quad(q):
        return index_of_axes(mesh, (q // ncore, lon, lat, lax.rem(q, ncore)))

    def others(count, me, do):
        def step(q, _):
            pl.when(q != me)(lambda: do(q))
            return 0

        lax.fori_loop(0, count, step, 0)

    loads = [
        pltpu.make_async_copy(src, dst, lsem.at[j])
        for j, (src, dst) in enumerate(
            ((state, st_in), (adj, adj_in), (wts, wts_in), (slp, slp_in))
        )
    ]
    for load in loads:
        load.start()
    barrier = pltpu.get_barrier_semaphore()

    def greet(device):
        pl.semaphore_signal(barrier, inc=1, device_id=device, device_id_type=MESH)

    others(nplane, here, lambda q: greet(in_plane(q)))
    others(nquad, corner, lambda q: greet(in_quad(q)))
    pl.semaphore_wait(barrier, nplane + nquad - 2)

    def flag(src, table, me, to, q, send, recv):
        return pltpu.make_async_remote_copy(
            src_ref=src, dst_ref=table.at[me], send_sem=send.at[q], recv_sem=recv.at[me],
            device_id=to(q), device_id_type=MESH,
        )

    def flag_in(src, table, to, q, send, recv):
        return pltpu.make_async_remote_copy(
            src_ref=src, dst_ref=table.at[q], send_sem=send.at[q], recv_sem=recv.at[q],
            device_id=to(q), device_id_type=MESH,
        )

    others(nplane, here, lambda q: flag(mine, plane, here, in_plane, q, psem, qsem).start())
    plane[here] = mine[...]

    def groups():
        n = 0
        for k, step in enumerate(plan.near):
            for off, size, far in plan.chunks[k]:
                rows = pl.ds(plan.bases[k] + off, size)
                send, get = plan.exists(lat, step[0]), plan.exists(lat, -step[0])
                if far is not None:
                    send = send & (polar == far)
                    get = get & (plan.polar(lat - step[0]) == far)
                yield n, k, step, off, rows, send, get
                n += 1

    def outgoing(n, step, rows):
        device = index_of_axes(mesh, plan.device(step))
        pairs = [
            (pwts.at[rows], rwts.at[rows, core]),
            (pslp.at[rows], rslp.at[rows, core]),
            (padj.at[rows], radj.at[rows]),
        ]
        return [
            pltpu.make_async_remote_copy(
                src_ref=src, dst_ref=dst, send_sem=ssem.at[n, j], recv_sem=rsem.at[n, j],
                device_id=device, device_id_type=MESH,
            )
            for j, (src, dst) in enumerate(pairs)
        ]

    def table(k, step):
        return pltpu.make_async_remote_copy(
            src_ref=pdest.at[k], dst_ref=rdest.at[k],
            send_sem=ssem.at[plan.copies + k, 0], recv_sem=rsem.at[plan.copies + k, 0],
            device_id=index_of_axes(mesh, plan.device(step)), device_id_type=MESH,
        )

    def passed(n, rows):
        return [
            pltpu.make_async_remote_copy(
                src_ref=ref.at[rows, core], dst_ref=ref.at[rows, core],
                send_sem=fsem.at[n, j], recv_sem=gsem.at[n, j],
                device_id=partner, device_id_type=MESH,
            )
            for j, ref in enumerate((rwts, rslp))
        ]

    for n, k, step, off, rows, send, get in groups():

        @pl.when(send)
        def _():
            if off == 0:
                table(k, step).start()
            for copy in outgoing(n, step, rows)[:2]:
                copy.start()

    for n, k, step, off, rows, send, get in groups():
        pl.when(send)(lambda: outgoing(n, step, rows)[2].start())

    others(nplane, here, lambda q: flag_in(mine, plane, in_plane, q, psem, qsem).wait_recv())
    both[...] = jnp.max(plane[...], axis=0)
    others(nquad, corner, lambda q: flag(both, quad, corner, in_quad, q, usem, vsem).start())
    quad[corner] = both[...]

    total[...] = jnp.zeros_like(total)
    for load in loads:
        load.wait()

    def local(t, _):
        a, block = adj_in[t], own[t]
        contrib = jnp.dot(a, wts_in[t], preferred_element_type=jnp.float32)
        for b in range(total.shape[0]):
            total[b] += jnp.where(block == b, contrib, 0.0)
        deriv = lax.dot_general(
            st_in[jnp.maximum(block, 0)].reshape(total.shape[1:]), slp_in[t],
            (((1,), (1,)), ((), ())), preferred_element_type=jnp.float32,
        )
        row = jnp.sum(deriv * a.astype(jnp.float32), axis=0, keepdims=True)
        wind[t] = jnp.where(block >= 0, row, 0.0)
        return 0

    lax.fori_loop(0, adj_in.shape[0], local, 0)
    store = pltpu.make_async_copy(total, home, lsem.at[len(loads)])
    store.start()

    for n, k, step, off, rows, send, get in groups():

        @pl.when(get)
        def _():
            arrive, on = outgoing(n, step, rows), passed(n, rows)
            for j in range(2):
                arrive[j].wait_recv()
                on[j].start()

    others(nquad, corner, lambda q: flag_in(both, quad, in_quad, q, usem, vsem).wait())
    others(nplane, here, lambda q: flag_in(mine, plane, in_plane, q, psem, qsem).wait_send())
    over[0] = jnp.max(quad[...])
    store.wait()

    for n, k, step, off, rows, send, get in groups():

        @pl.when(get)
        def _():
            if off == 0:
                table(k, step).wait_recv()
            outgoing(n, step, rows)[2].wait_recv()
            for copy in passed(n, rows):
                copy.wait()

        @pl.when(send)
        def _():
            if off == 0:
                table(k, step).wait_send()
            for copy in outgoing(n, step, rows):
                copy.wait_send()


def work_kernel(
    plan, rdest, state, home, radj, rwts, rslp, src_adj, wind,
    total, adj_in, wts_in, slp_in, sems, hsem,
):
    lat = lax.axis_index("lat")
    base = pltpu.make_async_copy(home, total, hsem.at[0])

    def copies(t):
        pairs = ((radj, adj_in), (rwts, wts_in), (rslp, slp_in))
        return [
            pltpu.make_async_copy(src.at[t], dst.at[t], sems.at[t, j])
            for j, (src, dst) in enumerate(pairs)
        ]

    def every(do):
        for k, step in enumerate(plan.near):
            came = jnp.where(plan.exists(lat, -step[0]), rdest[k, REGION], 0)

            def arrived(i, _, k=k):
                do(rdest[k, i], plan.bases[k] + i, k * REGION + i)
                return 0

            lax.fori_loop(0, came, arrived, 0)

    def begin(block, t, row):
        for copy in copies(t):
            copy.start()

    def tile(block, t, row):
        for copy in copies(t):
            copy.wait()
        a = adj_in[t]
        total[block] += jnp.dot(a, wts_in[t], preferred_element_type=jnp.float32)
        deriv = lax.dot_general(
            state[block].reshape(total.shape[1:]), slp_in[t], (((1,), (1,)), ((), ())),
            preferred_element_type=jnp.float32,
        )
        wind[row] = jnp.sum(deriv * a.astype(jnp.float32), axis=0, keepdims=True)

    base.start()
    every(begin)
    wind[...] = jnp.zeros_like(wind)
    base.wait()
    every(tile)

    def give(b, _):
        src_adj[b] = total[b].reshape(src_adj.shape[1:])
        return 0

    lax.fori_loop(0, total.shape[0], give, 0)


def wind_kernel(plan, mesh, ntile, slot, wind, own_wind, out, held, ssem, rsem):
    lat, core = lax.axis_index("lat"), lax.axis_index("lev")
    held[...] = jnp.zeros_like(held)
    here = (lax.axis_index("grp"), lax.axis_index("lon"), lat)
    partner = index_of_axes(mesh, here + (1 - core,))
    barrier = pltpu.get_barrier_semaphore()
    pl.semaphore_signal(barrier, inc=1, device_id=partner, device_id_type=MESH)
    expected = 1
    for step in plan.near:
        there = plan.exists(lat, step[0])
        expected = expected + 2 * there.astype(jnp.int32)

        @pl.when(there)
        def _(step=step):
            for c in range(2):
                pl.semaphore_signal(
                    barrier, inc=1,
                    device_id=index_of_axes(mesh, plan.device(step, 1, c)), device_id_type=MESH,
                )

    pl.semaphore_wait(barrier, expected)

    def back(k, step, c):
        rows = pl.ds(k * REGION, REGION)
        to = core if c == 0 else 1 - core
        return pltpu.make_async_remote_copy(
            src_ref=wind.at[rows], dst_ref=held.at[core, rows],
            send_sem=ssem.at[k, c], recv_sem=rsem.at[k, c],
            device_id=index_of_axes(mesh, plan.device(step, -1, to)), device_id_type=MESH,
        )

    mine = pl.ds(plan.count * REGION, ntile)
    across = pltpu.make_async_remote_copy(
        src_ref=own_wind, dst_ref=held.at[core, mine],
        send_sem=ssem.at[plan.count, 0], recv_sem=rsem.at[plan.count, 0],
        device_id=partner, device_id_type=MESH,
    )
    for k, step in enumerate(plan.near):

        @pl.when(plan.exists(lat, -step[0]))
        def _(k=k, step=step):
            for c in range(2):
                back(k, step, c).start()

    across.start()
    held[core, mine] = own_wind[...]
    across.wait()
    for k, step in enumerate(plan.near):

        @pl.when(plan.exists(lat, step[0]))
        def _(k=k, step=step):
            for c in range(2):
                back(k, step, c).wait_recv()

        @pl.when(plan.exists(lat, -step[0]))
        def _(k=k, step=step):
            for c in range(2):
                back(k, step, c).wait_send()

    for t in range(ntile):
        out[t] = held[0, slot[t]] + held[1, slot[t]]


def on_device(mesh, state, adj_in, weights, slopes, dep_lat, dep_lon):
    rows, cols, levels, fields, cells = state.shape
    tpb, points = adj_in.shape[2], adj_in.shape[-1]
    channels, ntile, half = levels * fields, rows * cols * tpb, points // 2
    plan = Plan(mesh, ntile)
    plan.copies = sum(len(c) for c in plan.chunks)
    f32, bf16, i32 = jnp.float32, jnp.bfloat16, jnp.int32
    shape = jax.ShapeDtypeStruct
    anyref = pl.BlockSpec(memory_space=pl.ANY)
    smem = pl.BlockSpec(memory_space=pltpu.SMEM)
    vmem = pl.BlockSpec(memory_space=pltpu.VMEM)
    params = functools.partial(pltpu.CompilerParams, vmem_limit_bytes=48 * 2**20)

    st = state.reshape(rows * cols, levels, fields, cells)
    adj = adj_in.reshape(ntile, channels, points)
    wts = weights.reshape(ntile, points, cells)
    slp = slopes.reshape(ntile, points, cells)

    padj, pwts, pslp, dest, own, slot, mine = pl.pallas_call(
        functools.partial(pack_kernel, plan, (rows, cols, tpb, half)),
        out_shape=(
            shape((plan.slots, channels, points), bf16),
            shape((plan.slots, half, cells), bf16),
            shape((plan.slots, half, cells), bf16),
            shape((plan.count, REGION + 1), i32),
            shape((ntile,), i32),
            shape((ntile,), i32),
            shape((8, 128), i32),
        ),
        in_specs=[smem, anyref, anyref, anyref],
        out_specs=(anyref, anyref, anyref, smem, smem, smem, vmem),
        scratch_shapes=[pltpu.SMEM((1,), i32), pltpu.SMEM((plan.count + ntile,), i32), pltpu.SemaphoreType.DMA((ntile, 3))],
        compiler_params=params(),
        name="pack",
    )((dep_lat + HW) * 8 + dep_lon + HW, adj, wts, slp)

    tables = jnp.broadcast_to(
        jnp.pad(dest, ((0, 0), (0, 127 - REGION)))[:, None, :], (plan.count, 8, 128)
    )
    groups = plan.copies + plan.count
    nplane = plan.nlon * plan.nlat
    nquad = mesh.shape["grp"] * mesh.shape["lev"]
    dma = pltpu.SemaphoreType.DMA
    radj, rwts, rslp, rdest, over, home, own_wind = pl.pallas_call(
        functools.partial(send_kernel, plan, mesh),
        out_shape=(
            shape((plan.slots, channels, points), bf16),
            shape((plan.slots, 2, half, cells), bf16),
            shape((plan.slots, 2, half, cells), bf16),
            shape((plan.count, 8, 128), i32),
            shape((1,), i32),
            shape((rows * cols, channels, cells), f32),
            shape((ntile, 1, points), f32),
        ),
        in_specs=[anyref] * 4 + [vmem, smem] + [anyref] * 4,
        out_specs=(anyref,) * 4 + (smem, anyref, vmem),
        scratch_shapes=[
            pltpu.VMEM(st.shape, bf16),
            pltpu.VMEM(adj.shape, bf16),
            pltpu.VMEM(wts.shape, bf16),
            pltpu.VMEM(slp.shape, bf16),
            pltpu.VMEM((rows * cols, channels, cells), f32),
            dma((5,)),
            pltpu.VMEM((nplane, 8, 128), i32),
            pltpu.VMEM((8, 128), i32),
            pltpu.VMEM((nquad, 8, 128), i32),
            pltpu.SemaphoreType.DMA((groups, 3)),
            pltpu.SemaphoreType.DMA((groups, 3)),
            pltpu.SemaphoreType.DMA((plan.copies, 2)),
            pltpu.SemaphoreType.DMA((plan.copies, 2)),
            dma((nplane,)), dma((nplane,)), dma((nquad,)), dma((nquad,)),
        ],
        compiler_params=params(collective_id=1, has_side_effects=True),
        name="send_tiles",
    )(padj, pwts, pslp, tables, mine, own, st, adj, wts, slp)

    rdest = rdest[:, 0, : REGION + 1]

    def owner_path(_):
        total = plan.count * REGION
        src_adj, wind = pl.pallas_call(
            functools.partial(work_kernel, plan),
            out_shape=(
                shape((rows * cols, levels, fields, cells), f32),
                shape((total, 1, points), f32),
            ),
            in_specs=[smem, vmem] + [anyref] * 4,
            out_specs=(vmem, vmem),
            scratch_shapes=[
                pltpu.VMEM((rows * cols, channels, cells), f32),
                pltpu.VMEM((plan.slots, channels, points), bf16),
                pltpu.VMEM((plan.slots, points, cells), bf16),
                pltpu.VMEM((plan.slots, points, cells), bf16),
                dma((plan.slots, 3)),
                dma((1,)),
            ],
            compiler_params=params(),
            name="tile_products",
        )(
            rdest, st, home, radj,
            rwts.reshape(plan.slots, points, cells), rslp.reshape(plan.slots, points, cells),
        )
        wind = pl.pallas_call(
            functools.partial(wind_kernel, plan, mesh, ntile),
            out_shape=shape((ntile, 1, points), f32),
            in_specs=[smem, vmem, vmem],
            out_specs=vmem,
            scratch_shapes=[
                pltpu.VMEM((2, total + ntile, 1, points), f32),
                pltpu.SemaphoreType.DMA((plan.count + 1, 2)),
                pltpu.SemaphoreType.DMA((plan.count + 1, 2)),
            ],
            compiler_params=params(collective_id=2, has_side_effects=True),
            name="wind_rows",
        )(slot, wind, own_wind)
        return src_adj, wind.reshape(ntile, points)

    def general_path(_):
        return halo_path(state, adj_in, weights, slopes, dep_lat, dep_lon)

    src_adj, wind = lax.cond(over[0] > 0, general_path, owner_path, 0)
    return (
        src_adj.reshape(rows, cols, levels, fields, cells),
        wind.reshape(rows, cols, tpb, points),
    )


def solution(mesh):
    placed = (
        P(("grp", "lat"), "lon", "lev", None, None),
        P(("grp", "lat"), "lon", None, "lev", None, None),
        P(("grp", "lat"), "lon", None, None, None),
        P(("grp", "lat"), "lon", None, None, None),
        P(("grp", "lat"), "lon", None),
        P(("grp", "lat"), "lon", None),
    )
    return jax.shard_map(
        functools.partial(on_device, mesh),
        mesh=mesh,
        in_specs=placed,
        out_specs=(
            P(("grp", "lat"), "lon", "lev", None, None),
            P(("grp", "lat"), "lon", None, None),
        ),
        check_vma=False,
    )
```
